1024 devices in a mesh: dp: 8 (over x_hi, core), mp: 128 (over y, z, x_lo).
Axes of the slice: x: 8 (x_hi: 4, x_lo: 2; x = x_hi * 2 + x_lo), y: 8, z: 8, core: 2. Of those that a mesh axis runs over, the one named last changes fastest.
Arguments:
- patches: bfloat16 [8, 192, 6144], P('dp', None, 'mp'), may hold values from -550 to 550
- keep_list: int32 [8, 128], P('dp'), may hold values from 0 to 191, as said below
- norm_gain: float32 [6144], replicated, may hold values from 0.1 to 1.9
- up_weight: bfloat16 [6144, 24576], P(None, 'mp'), may hold values from -0.078125 to 0.078125
- hidden_grad: bfloat16 [8, 128, 24576], P('dp', None, 'mp'), may hold values from -0.3984375 to 0.3984375
Outputs:
- hidden: bfloat16 [8, 128, 24576], P('dp', None, 'mp')
- weight_grad: float32 [6144, 24576], P('dp', 'mp')
The draws below stay inside these ranges and needn't reach their ends.
Inputs may be any that keep to these rules, and one draw needn't show every extreme that they name: `keep_list`: each image's list is increasing and always holds 0 and 191.
All inputs are finite; a program needn't handle non-finite values.
Results may differ from the reference program's by a relative error of at most 0.0055.
Values may be sent and summed in bfloat16 or wider, within the bound.
No kernel may reach another device: no remote copies, remote signals or barrier semaphores. Data moves between devices by JAX's collectives and lax.ppermute only.
A program may use at most 32 MiB of HBM per device.

```python
import math
import jax
import jax.numpy as jnp
from jax import lax

D = 6144
FF = 24576
PATCHES = 192
KEEP = 128
IMAGES = 8


def draw_patches(key, part):
    key = jax.random.fold_in(key, 5)
    base_key, column_key, row_key = jax.random.split(key, 3)
    base = jnp.clip(jax.random.normal(base_key, (IMAGES, PATCHES, D), jnp.float32), -5.0, 5.0)
    column_scale = jnp.exp(jax.random.uniform(column_key, (D,), jnp.float32, 0.0, math.log(10.0)))
    row_scale = jnp.exp(jax.random.uniform(row_key, (IMAGES, PATCHES, 1), jnp.float32, 0.0, math.log(10.0)))
    values = row_scale * base * column_scale
    return values.astype(jnp.bfloat16)


def draw_keep_list(key, part):
    key = jax.random.fold_in(key, 11)
    positions = jnp.arange(PATCHES, dtype=jnp.int32)[None, :]
    scores = jax.random.randint(key, (IMAGES, PATCHES), 0, 2 ** 20) * PATCHES + positions
    forced = jnp.logical_or(positions == 0, positions == PATCHES - 1)
    scores = jnp.where(forced, 2 ** 20 * PATCHES + positions, scores)
    top_values, picked = lax.top_k(scores, KEEP)
    return jnp.sort(picked.astype(jnp.int32), axis=1).astype(jnp.int32)


def steps_of(stream_key, shape, pieces, least, top_value):
    factor_of = 1.0
    for position, blocks in pieces:
        heights = jax.random.uniform(jax.random.fold_in(jax.random.fold_in(stream_key, 6), position), (blocks,), jnp.float32, least / len(pieces), top_value / len(pieces))
        factor_of = factor_of * jnp.repeat(jnp.exp(heights), shape[position] // blocks).reshape((-1,) + (1,) * (len(shape) - 1 - position))
    return factor_of


def scatter_about(rng, dims, scale, limit, cuts=(), held_as=jnp.bfloat16):
    entries = jax.random.normal(rng, dims, jnp.float32) * scale
    if len(cuts) > 0:
        entries = steps_of(rng, dims, cuts, -0.22, 0.18) * entries
    return jnp.clip(entries, min=-limit, max=limit).astype(held_as)


def setup_inputs(seed: int = 0) -> dict:
    keys = jax.random.split(jax.random.key(seed), 6)
    patches = draw_patches(jax.random.fold_in(keys[5], 71), 0)
    keep_list = draw_keep_list(jax.random.fold_in(keys[5], 71), 0)
    norm_gain = jnp.clip(1.0 + 0.18 * jax.random.normal(keys[2], (D,), jnp.float32), 0.1, 1.9)
    up_weight = scatter_about(keys[3], (D, FF), D ** -0.5, 0.078125, ((1, 128),))
    hidden_grad = scatter_about(keys[4], (IMAGES, KEEP, FF), 0.05, 0.3984375, ((0, 8), (2, 128)))
    return dict(patches=patches, keep_list=keep_list, norm_gain=norm_gain, up_weight=up_weight, hidden_grad=hidden_grad)


epsilon = 1e-06

def normalize(tokens, norm_gain):
    values = tokens.astype(jnp.float32)
    average = lax.optimization_barrier(jnp.mean(values, axis=-1, keepdims=True))
    centered = values - average
    variance = lax.optimization_barrier(jnp.mean(centered * centered, axis=-1, keepdims=True))
    return (centered * lax.rsqrt(variance + epsilon) * norm_gain.astype(jnp.float32)).astype(jnp.bfloat16)

def gelu_pair(preact):
    normal_cdf = 0.5 * (1.0 + jax.scipy.special.erf(preact * 0.7071067811865476))
    density = jnp.exp(-0.5 * preact * preact) * 0.3989422804014327
    return (preact * normal_cdf, normal_cdf + preact * density)

def reference(patches, keep_list, norm_gain, up_weight, hidden_grad):
    selected = jnp.take_along_axis(patches, keep_list[:, :, None], axis=1)
    normed = normalize(selected, norm_gain)
    flat_normed = normed.reshape(IMAGES * KEEP, D)
    preact = jnp.dot(flat_normed, up_weight, preferred_element_type=jnp.float32)
    activated, slope_full = gelu_pair(preact)
    hidden = activated.astype(jnp.bfloat16).reshape(IMAGES, KEEP, FF)
    flat_grad = hidden_grad.reshape(IMAGES * KEEP, FF).astype(jnp.float32)
    slope_rows = (flat_grad * slope_full).astype(jnp.bfloat16)
    weight_grad = lax.dot_general(flat_normed, slope_rows, (((0,), (0,)), ((), ())), preferred_element_type=jnp.float32)
    return (hidden, weight_grad)
```

```python
import functools

import jax
import jax.numpy as jnp
from jax import lax
from jax.experimental import pallas as pl
from jax.experimental.pallas import tpu as pltpu
from jax.sharding import PartitionSpec as P


epsilon = 1e-06
D = 6144
KEEP = 128
BF = jnp.bfloat16
F32 = jnp.float32
AXES = ("dp", "mp")


def flat(x_hi, core, y, z, x_lo):
    return (x_hi * 2 + core) * 128 + (y % 8) * 16 + (z % 8) * 2 + x_lo


def everyone():
    for x_hi in range(4):
        for core in range(2):
            for y in range(8):
                for z in range(8):
                    for x_lo in range(2):
                        yield x_hi, core, y, z, x_lo


def ring_pairs(step):
    pairs = []
    for x_hi, core, y, z, x_lo in everyone():
        to = (y + step, z) if core == 0 else (y, z + step)
        pairs.append((flat(x_hi, core, y, z, x_lo), flat(x_hi, core, to[0], to[1], x_lo)))
    return pairs


def swap_pairs():
    return [
        (flat(x_hi, core, y, z, x_lo), flat(y // 2, y % 2, x_hi * 2 + core, z, x_lo))
        for x_hi, core, y, z, x_lo in everyone()
    ]


def first_groups():
    groups = []
    for x_hi in range(4):
        for core in range(2):
            for fixed in range(8):
                groups.append(
                    [
                        flat(x_hi, core, *((fixed, run) if core == 0 else (run, fixed)), x_lo)
                        for run in range(8)
                        for x_lo in range(2)
                    ]
                )
    return groups


def gelu_pair(preact):
    normal_cdf = 0.5 * (1.0 + lax.erf(preact * 0.7071067811865476))
    density = jnp.exp(-0.5 * preact * preact) * 0.3989422804014327
    return (preact * normal_cdf, normal_cdf + preact * density)


def tiles(where, pieces, part):
    me = where[1]
    for k, refs in enumerate(pieces):
        shift = (0, -1, -2, -3, 1, 2, 3, 4)[k]
        ring = lax.rem(me + (shift + 8), 8)
        for j in range(8):
            for half in range(2):
                if len(refs) == 1:
                    yield refs[0].at[2 * j + half, part], ring, j, half
                else:
                    yield refs[j // 4].at[2 * (j % 4) + half, part], ring, j, half


def forward_kernel(where, *refs):
    pieces = [refs[k : k + 1] for k in range(7)] + [refs[7:9]]
    weight, gain, hidden_grad, hidden, payload, rows = refs[9:]
    on_y = where[0] == 0
    total = jnp.zeros((8, KEEP), F32)
    for tile, ring, j, half in tiles(where, pieces, 0):
        value = tile[...]
        place = jnp.where(on_y, ring * 768 + j * 96, j * 768 + ring * 96) + half * 48
        rows[pl.ds(pl.multiple_of(place, 16), 48), :] = value
        total += jnp.sum(value.astype(F32).reshape(6, 8, KEEP), axis=0)
    average = jnp.sum(total, axis=0, keepdims=True) * (1.0 / D)
    total = jnp.zeros((8, KEEP), F32)
    for start in range(0, D, 256):
        centered = rows[start : start + 256, :].astype(F32) - average
        total += jnp.sum((centered * centered).reshape(32, 8, KEEP), axis=0)
    variance = jnp.sum(total, axis=0, keepdims=True) * (1.0 / D)
    scale = lax.rsqrt(variance + epsilon)
    preact = jnp.zeros((192, KEEP), F32)
    for start in range(0, D, 256):
        centered = rows[start : start + 256, :].astype(F32) - average
        normed = (centered * scale * gain[start : start + 256, :]).astype(BF)
        preact += jnp.dot(weight[:, start : start + 256], normed, preferred_element_type=F32)
    activated, slope_full = gelu_pair(preact)
    hidden[...] = activated.astype(BF)
    payload[0:192, :] = (hidden_grad[...].astype(F32) * slope_full).astype(BF)
    lines = []
    for value in (average, scale):
        for _ in range(3):
            top = value.astype(BF).astype(F32)
            lines.append(top)
            value = value - top
    lines.append(jnp.zeros((10, KEEP), F32))
    payload[192:208, :] = jnp.concatenate(lines, axis=0).astype(BF)


def grad_kernel(where, *refs):
    pieces = [refs[k : k + 1] for k in range(7)] + [refs[7:9]]
    payload, gain, out, normed, slopes, averages, scales = refs[9:]
    on_y = where[0] == 0
    for image in range(8):
        ref = payload.at[image % 2, image // 2]
        slopes[:, image * KEEP : (image + 1) * KEEP] = ref[0:192, :]
        lines = ref[192:208, :].astype(F32)
        averages[image : image + 1, :] = lines[0:1] + lines[1:2] + lines[2:3]
        scales[image : image + 1, :] = lines[3:4] + lines[4:5] + lines[5:6]
    for tile, ring, j, half in tiles(where, pieces, 1):
        image = jnp.where(on_y, ring, j)
        place = pl.multiple_of(jnp.where(on_y, j * 96, ring * 96) + half * 48, 16)
        centered = tile[...].astype(F32) - averages[pl.ds(image, 1), :]
        value = centered * scales[pl.ds(image, 1), :] * gain[pl.ds(place, 48), :]
        normed[pl.ds(place, 48), pl.ds(pl.multiple_of(image * KEEP, KEEP), KEEP)] = value.astype(BF)
    out[...] = lax.dot_general(
        slopes[...], normed[...], (((1,), (1,)), ((), ())), preferred_element_type=F32
    )


VMEM = pl.BlockSpec(memory_space=pltpu.VMEM)
SMEM = pl.BlockSpec(memory_space=pltpu.SMEM)


def shards(patches, keep_list, norm_gain, up_weight, hidden_grad):
    dp, mp = lax.axis_index("dp"), lax.axis_index("mp")
    core = dp % 2
    where = jnp.stack([core, jnp.where(core == 0, mp // 16, (mp // 2) % 8)]).astype(jnp.int32)
    gain_all = jnp.broadcast_to(norm_gain[:, None], (D, KEEP))
    gain_block = jnp.broadcast_to(lax.dynamic_slice(norm_gain, (dp * 768,), (768,))[:, None], (768, KEEP))

    picked = (lax.broadcasted_iota(jnp.int32, (192, KEEP), 0) == keep_list).astype(BF)
    own = jnp.dot(patches[0].T, picked, preferred_element_type=F32).astype(BF)
    other = lax.ppermute(own, AXES, swap_pairs())
    both = jnp.broadcast_to(jnp.stack([own, other])[None], (16, 2, 48, KEEP))
    both = lax.all_to_all(both, AXES, 0, 0, axis_index_groups=first_groups())
    ahead = functools.partial(lax.ppermute, axis_name=AXES, perm=ring_pairs(1))
    back = functools.partial(lax.ppermute, axis_name=AXES, perm=ring_pairs(-1))
    f1, b1 = ahead(both), back(both)
    f2, b2 = ahead(f1), back(b1)
    f3, b3 = ahead(f2), back(b2)
    f4, b4 = ahead(f3[:8]), back(b3[8:])
    pieces = (both, f1, f2, f3, b1, b2, b3, f4, b4)

    hidden, payload = pl.pallas_call(
        forward_kernel,
        out_shape=(jax.ShapeDtypeStruct((192, KEEP), BF), jax.ShapeDtypeStruct((208, KEEP), BF)),
        in_specs=[SMEM] + [VMEM] * 12,
        out_specs=(VMEM, VMEM),
        scratch_shapes=[pltpu.VMEM((D, KEEP), BF)],
        compiler_params=pltpu.CompilerParams(vmem_limit_bytes=24 * 2**20),
        name="forward",
    )(where, *pieces, up_weight.T, gain_all, hidden_grad[0].T)

    payload = lax.all_to_all(
        jnp.broadcast_to(payload[None], (4, 208, KEEP)), "dp", 0, 0, axis_index_groups=[[0, 2, 4, 6], [1, 3, 5, 7]]
    )
    payload = lax.all_gather(payload, "dp", axis_index_groups=[[0, 1], [2, 3], [4, 5], [6, 7]])

    grad = pl.pallas_call(
        grad_kernel,
        out_shape=jax.ShapeDtypeStruct((192, 768), F32),
        in_specs=[SMEM] + [VMEM] * 11,
        out_specs=VMEM,
        scratch_shapes=[
            pltpu.VMEM((768, 1024), BF),
            pltpu.VMEM((192, 1024), BF),
            pltpu.VMEM((8, KEEP), F32),
            pltpu.VMEM((8, KEEP), F32),
        ],
        compiler_params=pltpu.CompilerParams(vmem_limit_bytes=24 * 2**20),
        name="weight_grad",
    )(where, *pieces, payload, gain_block)
    return (hidden.T[None], grad.T)


def solution(mesh):
    placed = (P("dp", None, "mp"), P("dp", None), P(), P(None, "mp"), P("dp", None, "mp"))
    return jax.shard_map(
        shards,
        mesh=mesh,
        in_specs=placed,
        out_specs=(P("dp", None, "mp"), P("dp", "mp")),
        check_vma=False,
    )
```

```python
import functools

import jax
import jax.numpy as jnp
from jax import lax
from jax.experimental import pallas as pl
from jax.experimental.pallas import tpu as pltpu
from jax.sharding import PartitionSpec as P


epsilon = 1e-06
D = 6144
KEEP = 128
BF = jnp.bfloat16
F32 = jnp.float32
AXES = ("dp", "mp")


def flat(x_hi, core, y, z, x_lo):
    return (x_hi * 2 + core) * 128 + (y % 8) * 16 + (z % 8) * 2 + x_lo


def everyone():
    for x_hi in range(4):
        for core in range(2):
            for y in range(8):
                for z in range(8):
                    for x_lo in range(2):
                        yield x_hi, core, y, z, x_lo


def ring_pairs(step):
    pairs = []
    for x_hi, core, y, z, x_lo in everyone():
        to = (y + step, z) if core == 0 else (y, z + step)
        pairs.append((flat(x_hi, core, y, z, x_lo), flat(x_hi, core, to[0], to[1], x_lo)))
    return pairs


def swap_pairs():
    return [
        (flat(x_hi, core, y, z, x_lo), flat(y // 2, y % 2, x_hi * 2 + core, z, x_lo))
        for x_hi, core, y, z, x_lo in everyone()
    ]


def ring_groups():
    groups = []
    for x_hi in range(4):
        for core in range(2):
            for fixed in range(8):
                for x_lo in range(2):
                    groups.append(
                        [
                            flat(x_hi, core, *((run, fixed) if core == 0 else (fixed, run)), x_lo)
                            for run in range(8)
                        ]
                    )
    return groups


def x_pairs(step):
    return [
        (flat(x_hi, core, y, z, x_lo), flat((x_hi + step) % 4, core, y, z, x_lo))
        for x_hi, core, y, z, x_lo in everyone()
    ]


def first_groups():
    groups = []
    for x_hi in range(4):
        for core in range(2):
            for fixed in range(8):
                groups.append(
                    [
                        flat(x_hi, core, *((fixed, run) if core == 0 else (run, fixed)), x_lo)
                        for run in range(8)
                        for x_lo in range(2)
                    ]
                )
    return groups


def gelu_pair(preact):
    normal_cdf = 0.5 * (1.0 + lax.erf(preact * 0.7071067811865476))
    density = jnp.exp(-0.5 * preact * preact) * 0.3989422804014327
    return (preact * normal_cdf, normal_cdf + preact * density)


def tiles(me, pieces):
    for k, refs in enumerate(pieces):
        shift = (0, -1, -2, -3, 1, 2, 3, 4)[k]
        ring = lax.rem(me + (shift + 8), 8)
        for j in range(8):
            for half in range(2):
                ref, row = (refs[0], j) if len(refs) == 1 else (refs[j // 4], j % 4)
                yield ref.at[2 * row + half], ring, j, half


def forward_kernel(where, *refs):
    pieces = [refs[k : k + 1] for k in range(7)] + [refs[7:9]]
    weight, gain, hidden_grad, hidden, payload, rows = refs[9:]
    on_y = where[0] == 0
    total = jnp.zeros((8, KEEP), F32)
    for tile, ring, j, half in tiles(where[1], pieces):
        value = tile[...]
        place = jnp.where(on_y, ring * 768 + j * 96, j * 768 + ring * 96) + half * 48
        rows[pl.ds(pl.multiple_of(place, 16), 48), :] = value
        total += jnp.sum(value.astype(F32).reshape(6, 8, KEEP), axis=0)
    average = jnp.sum(total, axis=0, keepdims=True) * (1.0 / D)
    total = jnp.zeros((8, KEEP), F32)
    for start in range(0, D, 256):
        centered = rows[start : start + 256, :].astype(F32) - average
        total += jnp.sum((centered * centered).reshape(32, 8, KEEP), axis=0)
    variance = jnp.sum(total, axis=0, keepdims=True) * (1.0 / D)
    scale = lax.rsqrt(variance + epsilon)
    preact = jnp.zeros((192, KEEP), F32)
    for start in range(0, D, 256):
        centered = rows[start : start + 256, :].astype(F32) - average
        normed = (centered * scale * gain[start : start + 256, :]).astype(BF)
        preact += jnp.dot(weight[:, start : start + 256], normed, preferred_element_type=F32)
    activated, slope_full = gelu_pair(preact)
    hidden[...] = activated.astype(BF)
    payload[0:192, :] = (hidden_grad[...].astype(F32) * slope_full).astype(BF)
    lines = []
    for value in (average, scale):
        for _ in range(3):
            top = value.astype(BF).astype(F32)
            lines.append(top)
            value = value - top
    lines.append(jnp.zeros((10, KEEP), F32))
    payload[192:208, :] = jnp.concatenate(lines, axis=0).astype(BF)


def grad_kernel(where, blocks, payload, gain, out, normed, slopes, averages, scales):
    on_y = where[0] == 0
    for image in range(8):
        ref = payload.at[image % 2, lax.rem(where[2] + (4 - image // 2), 4)]
        slopes[:, image * KEEP : (image + 1) * KEEP] = ref[0:192, :]
        lines = ref[192:208, :].astype(F32)
        averages[image : image + 1, :] = lines[0:1] + lines[1:2] + lines[2:3]
        scales[image : image + 1, :] = lines[3:4] + lines[4:5] + lines[5:6]
    for ring, j, half in ((ring, j, half) for ring in range(8) for j in range(8) for half in range(2)):
        image = jnp.where(on_y, ring, j)
        place = pl.multiple_of(jnp.where(on_y, j * 96, ring * 96) + half * 48, 16)
        centered = blocks[ring, 2 * j + half].astype(F32) - averages[pl.ds(image, 1), :]
        value = centered * scales[pl.ds(image, 1), :] * gain[pl.ds(place, 48), :]
        normed[pl.ds(place, 48), pl.ds(pl.multiple_of(image * KEEP, KEEP), KEEP)] = value.astype(BF)
    out[...] = lax.dot_general(
        slopes[...], normed[...], (((1,), (1,)), ((), ())), preferred_element_type=F32
    )


VMEM = pl.BlockSpec(memory_space=pltpu.VMEM)
SMEM = pl.BlockSpec(memory_space=pltpu.SMEM)


def shards(patches, keep_list, norm_gain, up_weight, hidden_grad):
    dp, mp = lax.axis_index("dp"), lax.axis_index("mp")
    core = dp % 2
    where = jnp.stack([core, jnp.where(core == 0, mp // 16, (mp // 2) % 8), dp // 2]).astype(jnp.int32)
    gain_all = jnp.broadcast_to(norm_gain[:, None], (D, KEEP))
    gain_block = jnp.broadcast_to(lax.dynamic_slice(norm_gain, (dp * 768,), (768,))[:, None], (768, KEEP))

    picked = (lax.broadcasted_iota(jnp.int32, (192, KEEP), 0) == keep_list).astype(BF)
    own = jnp.dot(patches[0].T, picked, preferred_element_type=F32).astype(BF)
    other = lax.ppermute(own, AXES, swap_pairs())
    both = jnp.broadcast_to(jnp.stack([own, other])[None], (16, 2, 48, KEEP))
    both = lax.all_to_all(both, AXES, 0, 0, axis_index_groups=first_groups())
    ahead = functools.partial(lax.ppermute, axis_name=AXES, perm=ring_pairs(1))
    back = functools.partial(lax.ppermute, axis_name=AXES, perm=ring_pairs(-1))
    blocks = lax.all_gather(both[:, 1], AXES, axis_index_groups=ring_groups())
    own = both[:, 0]
    f1, b1 = ahead(own), back(own)
    f2, b2 = ahead(f1), back(b1)
    f3, b3 = ahead(f2), back(b2)
    f4, b4 = ahead(f3[:8]), back(b3[8:])
    pieces = (own, f1, f2, f3, b1, b2, b3, f4, b4)

    hidden, payload = pl.pallas_call(
        forward_kernel,
        out_shape=(jax.ShapeDtypeStruct((192, KEEP), BF), jax.ShapeDtypeStruct((208, KEEP), BF)),
        in_specs=[SMEM] + [VMEM] * 12,
        out_specs=(VMEM, VMEM),
        scratch_shapes=[pltpu.VMEM((D, KEEP), BF)],
        compiler_params=pltpu.CompilerParams(vmem_limit_bytes=24 * 2**20),
        name="forward",
    )(where, *pieces, up_weight.T, gain_all, hidden_grad[0].T)

    payload = jnp.stack([payload] + [lax.ppermute(payload, AXES, x_pairs(step)) for step in (1, 2, 3)])
    payload = lax.all_gather(payload, "dp", axis_index_groups=[[0, 1], [2, 3], [4, 5], [6, 7]])

    grad = pl.pallas_call(
        grad_kernel,
        out_shape=jax.ShapeDtypeStruct((192, 768), F32),
        in_specs=[SMEM] + [VMEM] * 3,
        out_specs=VMEM,
        scratch_shapes=[
            pltpu.VMEM((768, 1024), BF),
            pltpu.VMEM((192, 1024), BF),
            pltpu.VMEM((8, KEEP), F32),
            pltpu.VMEM((8, KEEP), F32),
        ],
        compiler_params=pltpu.CompilerParams(vmem_limit_bytes=24 * 2**20),
        name="weight_grad",
    )(where, blocks, payload, gain_block)
    return (hidden.T[None], grad.T)


def solution(mesh):
    placed = (P("dp", None, "mp"), P("dp", None), P(), P(None, "mp"), P("dp", None, "mp"))
    return jax.shard_map(
        shards,
        mesh=mesh,
        in_specs=placed,
        out_specs=(P("dp", None, "mp"), P("dp", "mp")),
        check_vma=False,
    )
```

```python
import functools

import jax
import jax.numpy as jnp
from jax import lax
from jax.experimental import pallas as pl
from jax.experimental.pallas import tpu as pltpu
from jax.sharding import PartitionSpec as P


epsilon = 1e-06
D = 6144
KEEP = 128
BF = jnp.bfloat16
F32 = jnp.float32
AXES = ("dp", "mp")


def flat(x_hi, core, y, z, x_lo):
    return (x_hi * 2 + core) * 128 + (y % 8) * 16 + (z % 8) * 2 + x_lo


def everyone():
    for x_hi in range(4):
        for core in range(2):
            for y in range(8):
                for z in range(8):
                    for x_lo in range(2):
                        yield x_hi, core, y, z, x_lo


def ring_pairs(step):
    pairs = []
    for x_hi, core, y, z, x_lo in everyone():
        to = (y + step, z) if core == 0 else (y, z + step)
        pairs.append((flat(x_hi, core, y, z, x_lo), flat(x_hi, core, to[0], to[1], x_lo)))
    return pairs


def swap_pairs():
    return [
        (flat(x_hi, core, y, z, x_lo), flat(y // 2, y % 2, x_hi * 2 + core, z, x_lo))
        for x_hi, core, y, z, x_lo in everyone()
    ]


def first_groups():
    groups = []
    for x_hi in range(4):
        for core in range(2):
            for fixed in range(8):
                groups.append(
                    [
                        flat(x_hi, core, *((fixed, run) if core == 0 else (run, fixed)), x_lo)
                        for run in range(8)
                        for x_lo in range(2)
                    ]
                )
    return groups


def gelu_pair(preact):
    normal_cdf = 0.5 * (1.0 + lax.erf(preact * 0.7071067811865476))
    density = jnp.exp(-0.5 * preact * preact) * 0.3989422804014327
    return (preact * normal_cdf, normal_cdf + preact * density)


def tiles(me, pieces, part):
    for shift, ref in zip((0, -1, -2, -3, -4, 1, 2, 3), pieces):
        ring = lax.rem(me + (shift + 8), 8)
        for j in range(8):
            for half in range(2):
                yield ref.at[2 * j + half, part], ring, j, half


def spread_kernel(piece, gain, spread):
    for row in range(D // 128):
        spread[row * 128 : (row + 1) * 128, :] = jnp.broadcast_to(gain[row : row + 1, :], (128, KEEP)).T


def forward_kernel(where, *refs):
    pieces = refs[:8]
    weight, gain, hidden_grad, hidden, payload, rows = refs[8:]
    on_y = where[0] == 0
    total = jnp.zeros((8, KEEP), F32)
    for tile, ring, j, half in tiles(where[1], pieces, 0):
        value = tile[...]
        place = jnp.where(on_y, ring * 768 + j * 96, j * 768 + ring * 96) + half * 48
        rows[pl.ds(pl.multiple_of(place, 16), 48), :] = value
        total += jnp.sum(value.astype(F32).reshape(6, 8, KEEP), axis=0)
    average = jnp.sum(total, axis=0, keepdims=True) * (1.0 / D)
    total = jnp.zeros((8, KEEP), F32)
    for start in range(0, D, 256):
        centered = rows[start : start + 256, :].astype(F32) - average
        total += jnp.sum((centered * centered).reshape(32, 8, KEEP), axis=0)
    variance = jnp.sum(total, axis=0, keepdims=True) * (1.0 / D)
    scale = lax.rsqrt(variance + epsilon)
    preact = jnp.zeros((192, KEEP), F32)
    for start in range(0, D, 256):
        centered = rows[start : start + 256, :].astype(F32) - average
        normed = (centered * scale * gain[start : start + 256, :]).astype(BF)
        preact += jnp.dot(weight[:, start : start + 256], normed, preferred_element_type=F32)
    activated, slope_full = gelu_pair(preact)
    hidden[...] = activated.astype(BF)
    slope = (hidden_grad[...].astype(F32) * slope_full).astype(BF)
    lines = []
    for value in (average, scale):
        for _ in range(3):
            top = value.astype(BF).astype(F32)
            lines.append(top)
            value = value - top
    lines.append(jnp.zeros((10, KEEP), F32))
    lines = jnp.concatenate(lines, axis=0).astype(BF)
    for copy in range(4):
        payload[copy, 0:192, :] = slope
        payload[copy, 192:208, :] = lines


def grad_kernel(where, *refs):
    pieces = refs[:8]
    payload, gain, out, normed, slopes, averages, scales = refs[8:]
    first = where[2] * 768
    on_y = where[0] == 0
    for image in range(8):
        ref = payload.at[image % 2, image // 2]
        slopes[:, image * KEEP : (image + 1) * KEEP] = ref[0:192, :]
        lines = ref[192:208, :].astype(F32)
        averages[image : image + 1, :] = lines[0:1] + lines[1:2] + lines[2:3]
        scales[image : image + 1, :] = lines[3:4] + lines[4:5] + lines[5:6]
    for tile, ring, j, half in tiles(where[1], pieces, 1):
        image = jnp.where(on_y, ring, j)
        place = pl.multiple_of(jnp.where(on_y, j * 96, ring * 96) + half * 48, 16)
        centered = tile[...].astype(F32) - averages[pl.ds(image, 1), :]
        value = centered * scales[pl.ds(image, 1), :] * gain[pl.ds(pl.multiple_of(first + place, 16), 48), :]
        normed[pl.ds(place, 48), pl.ds(pl.multiple_of(image * KEEP, KEEP), KEEP)] = value.astype(BF)
    out[...] = lax.dot_general(
        slopes[...], normed[...], (((1,), (1,)), ((), ())), preferred_element_type=F32
    )


VMEM = pl.BlockSpec(memory_space=pltpu.VMEM)
SMEM = pl.BlockSpec(memory_space=pltpu.SMEM)


def shards(patches, keep_list, norm_gain, up_weight, hidden_grad):
    dp, mp = lax.axis_index("dp"), lax.axis_index("mp")
    core = dp % 2
    where = jnp.stack([core, jnp.where(core == 0, mp // 16, (mp // 2) % 8), dp]).astype(jnp.int32)

    picked = (lax.broadcasted_iota(jnp.int32, (192, KEEP), 0) == keep_list).astype(BF)
    own = jnp.dot(patches[0].T, picked, preferred_element_type=F32).astype(BF)
    other = lax.ppermute(own, AXES, swap_pairs())
    both = jnp.broadcast_to(jnp.stack([own, other])[None], (16, 2, 48, KEEP))
    both = lax.all_to_all(both, AXES, 0, 0, axis_index_groups=first_groups())
    ahead = functools.partial(lax.ppermute, axis_name=AXES, perm=ring_pairs(1))
    back = functools.partial(lax.ppermute, axis_name=AXES, perm=ring_pairs(-1))
    f1, b1 = ahead(both), back(both)
    f2, b2 = ahead(f1), back(b1)
    gain_all = pl.pallas_call(
        spread_kernel,
        out_shape=jax.ShapeDtypeStruct((D, KEEP), F32),
        in_specs=[pl.BlockSpec(memory_space=pl.ANY), VMEM],
        out_specs=VMEM,
        compiler_params=pltpu.CompilerParams(vmem_limit_bytes=24 * 2**20),
        cost_estimate=pl.CostEstimate(flops=2 * 2**30, bytes_accessed=8 * 2**20, transcendentals=0),
        name="spread",
    )(b2, norm_gain.reshape(D // 128, 128))
    f3, b3 = ahead(f2), back(b2)
    f4 = ahead(f3)
    pieces = (both, f1, f2, f3, f4, b1, b2, b3)

    hidden, payload = pl.pallas_call(
        forward_kernel,
        out_shape=(jax.ShapeDtypeStruct((192, KEEP), BF), jax.ShapeDtypeStruct((4, 208, KEEP), BF)),
        in_specs=[SMEM] + [VMEM] * 11,
        out_specs=(VMEM, VMEM),
        scratch_shapes=[pltpu.VMEM((D, KEEP), BF)],
        compiler_params=pltpu.CompilerParams(vmem_limit_bytes=24 * 2**20),
        name="forward",
    )(where, *pieces, up_weight.T, gain_all, hidden_grad[0].T)

    payload = lax.all_to_all(payload, "dp", 0, 0, axis_index_groups=[[0, 2, 4, 6], [1, 3, 5, 7]])
    payload = lax.all_gather(payload, "dp", axis_index_groups=[[0, 1], [2, 3], [4, 5], [6, 7]])

    grad = pl.pallas_call(
        grad_kernel,
        out_shape=jax.ShapeDtypeStruct((192, 768), F32),
        in_specs=[SMEM] + [VMEM] * 10,
        out_specs=VMEM,
        scratch_shapes=[
            pltpu.VMEM((768, 1024), BF),
            pltpu.VMEM((192, 1024), BF),
            pltpu.VMEM((8, KEEP), F32),
            pltpu.VMEM((8, KEEP), F32),
        ],
        compiler_params=pltpu.CompilerParams(vmem_limit_bytes=24 * 2**20),
        name="weight_grad",
    )(where, *pieces, payload, gain_all)
    return (hidden.T[None], grad.T)


def solution(mesh):
    placed = (P("dp", None, "mp"), P("dp", None), P(), P(None, "mp"), P("dp", None, "mp"))
    return jax.shard_map(
        shards,
        mesh=mesh,
        in_specs=placed,
        out_specs=(P("dp", None, "mp"), P("dp", "mp")),
        check_vma=False,
    )
```

```python
import jax
import jax.numpy as jnp
from jax import lax
from jax.experimental import pallas as pl
from jax.experimental.pallas import tpu as pltpu
from jax.sharding import PartitionSpec as P


epsilon = 1e-06
D = 6144
KEEP = 128
BF = jnp.bfloat16
F32 = jnp.float32
AXES = ("dp", "mp")


def flat(x_hi, core, y, z, x_lo):
    return (x_hi * 2 + core) * 128 + (y % 8) * 16 + (z % 8) * 2 + x_lo


def everyone():
    for x_hi in range(4):
        for core in range(2):
            for y in range(8):
                for z in range(8):
                    for x_lo in range(2):
                        yield x_hi, core, y, z, x_lo


def ring_pairs(step):
    pairs = []
    for x_hi, core, y, z, x_lo in everyone():
        to = (y + step, z) if core == 0 else (y, z + step)
        pairs.append((flat(x_hi, core, y, z, x_lo), flat(x_hi, core, to[0], to[1], x_lo)))
    return pairs


def swap_pairs():
    return [
        (flat(x_hi, core, y, z, x_lo), flat(y // 2, y % 2, x_hi * 2 + core, z, x_lo))
        for x_hi, core, y, z, x_lo in everyone()
    ]


def first_groups():
    groups = []
    for x_hi in range(4):
        for core in range(2):
            for fixed in range(8):
                groups.append(
                    [
                        flat(x_hi, core, *((fixed, run) if core == 0 else (run, fixed)), x_lo)
                        for run in range(8)
                        for x_lo in range(2)
                    ]
                )
    return groups


def gelu_pair(preact):
    normal_cdf = 0.5 * (1.0 + lax.erf(preact * 0.7071067811865476))
    density = jnp.exp(-0.5 * preact * preact) * 0.3989422804014327
    return (preact * normal_cdf, normal_cdf + preact * density)


def tiles(me, pieces, part):
    for shift, ref in zip((0, -1, -2, -3, -4, 1, 2, 3), pieces):
        ring = lax.rem(me + (shift + 8), 8)
        for j in range(8):
            for half in range(2):
                yield ref.at[2 * j + half, part], ring, j, half


def spread_kernel(piece, gain, spread):
    for row in range(D // 128):
        spread[row * 128 : (row + 1) * 128, :] = jnp.broadcast_to(gain[row : row + 1, :], (128, KEEP)).T


def forward_kernel(where, *refs):
    pieces = refs[:8]
    weight, gain, hidden_grad, hidden, payload, rows = refs[8:]
    on_y = where[0] == 0
    total = jnp.zeros((8, KEEP), F32)
    for tile, ring, j, half in tiles(where[1], pieces, 0):
        value = tile[...]
        place = jnp.where(on_y, ring * 768 + j * 96, j * 768 + ring * 96) + half * 48
        rows[pl.ds(pl.multiple_of(place, 16), 48), :] = value
        total += jnp.sum(value.astype(F32).reshape(6, 8, KEEP), axis=0)
    average = jnp.sum(total, axis=0, keepdims=True) * (1.0 / D)
    total = jnp.zeros((8, KEEP), F32)
    for start in range(0, D, 256):
        centered = rows[start : start + 256, :].astype(F32) - average
        total += jnp.sum((centered * centered).reshape(32, 8, KEEP), axis=0)
    variance = jnp.sum(total, axis=0, keepdims=True) * (1.0 / D)
    scale = lax.rsqrt(variance + epsilon)
    preact = jnp.zeros((192, KEEP), F32)
    for start in range(0, D, 256):
        centered = rows[start : start + 256, :].astype(F32) - average
        normed = (centered * scale * gain[start : start + 256, :]).astype(BF)
        preact += jnp.dot(weight[:, start : start + 256], normed, preferred_element_type=F32)
    activated, slope_full = gelu_pair(preact)
    hidden[...] = activated.astype(BF)
    slope = (hidden_grad[...].astype(F32) * slope_full).astype(BF)
    lines = []
    for value in (average, scale):
        for _ in range(3):
            top = value.astype(BF).astype(F32)
            lines.append(top)
            value = value - top
    lines.append(jnp.zeros((10, KEEP), F32))
    lines = jnp.concatenate(lines, axis=0).astype(BF)
    for copy in range(4):
        payload[copy, 0:192, :] = slope
        payload[copy, 192:208, :] = lines


def grad_kernel(where, *refs):
    pieces = refs[:8]
    payload, gain, out, normed, slopes, averages, scales = refs[8:]
    first = where[2] * 768
    on_y = where[0] == 0
    for image in range(8):
        ref = payload.at[image % 2, image // 2]
        slopes[:, image * KEEP : (image + 1) * KEEP] = ref[0:192, :]
        lines = ref[192:208, :].astype(F32)
        averages[image : image + 1, :] = lines[0:1] + lines[1:2] + lines[2:3]
        scales[image : image + 1, :] = lines[3:4] + lines[4:5] + lines[5:6]
    for tile, ring, j, half in tiles(where[1], pieces, 1):
        image = jnp.where(on_y, ring, j)
        place = pl.multiple_of(jnp.where(on_y, j * 96, ring * 96) + half * 48, 16)
        centered = tile[...].astype(F32) - averages[pl.ds(image, 1), :]
        value = centered * scales[pl.ds(image, 1), :] * gain[pl.ds(pl.multiple_of(first + place, 16), 48), :]
        normed[pl.ds(place, 48), pl.ds(pl.multiple_of(image * KEEP, KEEP), KEEP)] = value.astype(BF)
    out[...] = lax.dot_general(
        slopes[...], normed[...], (((1,), (1,)), ((), ())), preferred_element_type=F32
    )


VMEM = pl.BlockSpec(memory_space=pltpu.VMEM)
SMEM = pl.BlockSpec(memory_space=pltpu.SMEM)


def shards(patches, keep_list, norm_gain, up_weight, hidden_grad):
    dp, mp = lax.axis_index("dp"), lax.axis_index("mp")
    core = dp % 2
    where = jnp.stack([core, jnp.where(core == 0, mp // 16, (mp // 2) % 8), dp]).astype(jnp.int32)

    picked = (lax.broadcasted_iota(jnp.int32, (192, KEEP), 0) == keep_list).astype(BF)
    own = jnp.dot(patches[0].T, picked, preferred_element_type=F32).astype(BF)
    other = lax.ppermute(own, AXES, swap_pairs())
    both = jnp.broadcast_to(jnp.stack([own, other])[None], (16, 2, 48, KEEP))
    both = lax.all_to_all(both, AXES, 0, 0, axis_index_groups=first_groups())
    move = lambda piece, step: lax.ppermute(piece, AXES, ring_pairs(step))
    f2, b2 = move(both, 2), move(both, -2)
    f1, b1 = move(both, 1), move(both, -1)
    gain_all = pl.pallas_call(
        spread_kernel,
        out_shape=jax.ShapeDtypeStruct((D, KEEP), F32),
        in_specs=[pl.BlockSpec(memory_space=pl.ANY), VMEM],
        out_specs=VMEM,
        compiler_params=pltpu.CompilerParams(vmem_limit_bytes=24 * 2**20),
        cost_estimate=pl.CostEstimate(flops=2 * 2**30, bytes_accessed=8 * 2**20, transcendentals=0),
        name="spread",
    )(b2, norm_gain.reshape(D // 128, 128))
    f3, b3 = move(f2, 1), move(b2, -1)
    f4 = move(f3, 1)
    pieces = (both, f1, f2, f3, f4, b1, b2, b3)

    hidden, payload = pl.pallas_call(
        forward_kernel,
        out_shape=(jax.ShapeDtypeStruct((192, KEEP), BF), jax.ShapeDtypeStruct((4, 208, KEEP), BF)),
        in_specs=[SMEM] + [VMEM] * 11,
        out_specs=(VMEM, VMEM),
        scratch_shapes=[pltpu.VMEM((D, KEEP), BF)],
        compiler_params=pltpu.CompilerParams(vmem_limit_bytes=24 * 2**20),
        name="forward",
    )(where, *pieces, up_weight.T, gain_all, hidden_grad[0].T)

    payload = lax.all_to_all(payload, "dp", 0, 0, axis_index_groups=[[0, 2, 4, 6], [1, 3, 5, 7]])
    payload = lax.all_gather(payload, "dp", axis_index_groups=[[0, 1], [2, 3], [4, 5], [6, 7]])

    grad = pl.pallas_call(
        grad_kernel,
        out_shape=jax.ShapeDtypeStruct((192, 768), F32),
        in_specs=[SMEM] + [VMEM] * 10,
        out_specs=VMEM,
        scratch_shapes=[
            pltpu.VMEM((768, 1024), BF),
            pltpu.VMEM((192, 1024), BF),
            pltpu.VMEM((8, KEEP), F32),
            pltpu.VMEM((8, KEEP), F32),
        ],
        compiler_params=pltpu.CompilerParams(vmem_limit_bytes=24 * 2**20),
        name="weight_grad",
    )(where, *pieces, payload, gain_all)
    return (hidden.T[None], grad.T)


def solution(mesh):
    placed = (P("dp", None, "mp"), P("dp", None), P(), P(None, "mp"), P("dp", None, "mp"))
    return jax.shard_map(
        shards,
        mesh=mesh,
        in_specs=placed,
        out_specs=(P("dp", None, "mp"), P("dp", "mp")),
        check_vma=False,
    )
```

```python
import jax
import jax.numpy as jnp
from jax import lax
from jax.experimental import pallas as pl
from jax.experimental.pallas import tpu as pltpu
from jax.sharding import PartitionSpec as P


epsilon = 1e-06
D = 6144
KEEP = 128
BF = jnp.bfloat16
F32 = jnp.float32
AXES = ("dp", "mp")


def flat(x_hi, core, y, z, x_lo):
    return (x_hi * 2 + core) * 128 + (y % 8) * 16 + (z % 8) * 2 + x_lo


def everyone():
    for x_hi in range(4):
        for core in range(2):
            for y in range(8):
                for z in range(8):
                    for x_lo in range(2):
                        yield x_hi, core, y, z, x_lo


def ring_pairs(step):
    pairs = []
    for x_hi, core, y, z, x_lo in everyone():
        to = (y + step, z) if core == 0 else (y, z + step)
        pairs.append((flat(x_hi, core, y, z, x_lo), flat(x_hi, core, to[0], to[1], x_lo)))
    return pairs


def swap_pairs():
    return [
        (flat(x_hi, core, y, z, x_lo), flat(y // 2, y % 2, x_hi * 2 + core, z, x_lo))
        for x_hi, core, y, z, x_lo in everyone()
    ]


def first_groups():
    groups = []
    for x_hi in range(4):
        for core in range(2):
            for fixed in range(8):
                groups.append(
                    [
                        flat(x_hi, core, *((fixed, run) if core == 0 else (run, fixed)), x_lo)
                        for run in range(8)
                        for x_lo in range(2)
                    ]
                )
    return groups


def gelu_pair(preact):
    normal_cdf = 0.5 * (1.0 + lax.erf(preact * 0.7071067811865476))
    density = jnp.exp(-0.5 * preact * preact) * 0.3989422804014327
    return (preact * normal_cdf, normal_cdf + preact * density)


def tiles(me, pieces, part):
    for shift, ref in zip((0, -1, -2, -3, -4, 1, 2, 3), pieces):
        ring = lax.rem(me + (shift + 8), 8)
        for j in range(8):
            for half in range(2):
                yield ref.at[2 * j + half, part], ring, j, half


def spread_kernel(piece, gain, spread):
    for row in range(D // 128):
        spread[row * 128 : (row + 1) * 128, :] = jnp.broadcast_to(gain[row : row + 1, :], (128, KEEP)).T


def forward_kernel(where, *refs):
    pieces = refs[:8]
    weight, gain, hidden_grad, hidden, payload, rows = refs[8:]
    on_y = where[0] == 0
    total = jnp.zeros((8, KEEP), F32)
    for tile, ring, j, half in tiles(where[1], pieces, 0):
        value = tile[...]
        place = jnp.where(on_y, ring * 768 + j * 96, j * 768 + ring * 96) + half * 48
        rows[pl.ds(pl.multiple_of(place, 16), 48), :] = value
        total += jnp.sum(value.astype(F32).reshape(6, 8, KEEP), axis=0)
    average = jnp.sum(total, axis=0, keepdims=True) * (1.0 / D)
    total = jnp.zeros((8, KEEP), F32)
    for start in range(0, D, 256):
        centered = rows[start : start + 256, :].astype(F32) - average
        total += jnp.sum((centered * centered).reshape(32, 8, KEEP), axis=0)
    variance = jnp.sum(total, axis=0, keepdims=True) * (1.0 / D)
    scale = lax.rsqrt(variance + epsilon)
    preact = jnp.zeros((192, KEEP), F32)
    for start in range(0, D, 256):
        centered = rows[start : start + 256, :].astype(F32) - average
        normed = (centered * scale * gain[start : start + 256, :]).astype(BF)
        preact += jnp.dot(weight[:, start : start + 256], normed, preferred_element_type=F32)
    activated, slope_full = gelu_pair(preact)
    hidden[...] = activated.astype(BF)
    slope = (hidden_grad[...].astype(F32) * slope_full).astype(BF)
    lines = []
    for value in (average, scale):
        for _ in range(3):
            top = value.astype(BF).astype(F32)
            lines.append(top)
            value = value - top
    lines.append(jnp.zeros((10, KEEP), F32))
    lines = jnp.concatenate(lines, axis=0).astype(BF)
    for copy in range(4):
        payload[copy, 0:192, :] = slope
        payload[copy, 192:208, :] = lines


def grad_kernel(where, *refs):
    pieces = refs[:8]
    payload, gain, out, normed, slopes, averages, scales = refs[8:]
    first = where[2] * 768
    on_y = where[0] == 0
    for image in range(8):
        ref = payload.at[image % 2, image // 2]
        slopes[:, image * KEEP : (image + 1) * KEEP] = ref[0:192, :]
        lines = ref[192:208, :].astype(F32)
        averages[image : image + 1, :] = lines[0:1] + lines[1:2] + lines[2:3]
        scales[image : image + 1, :] = lines[3:4] + lines[4:5] + lines[5:6]
    for tile, ring, j, half in tiles(where[1], pieces, 1):
        image = jnp.where(on_y, ring, j)
        place = pl.multiple_of(jnp.where(on_y, j * 96, ring * 96) + half * 48, 16)
        centered = tile[...].astype(F32) - averages[pl.ds(image, 1), :]
        value = centered * scales[pl.ds(image, 1), :] * gain[pl.ds(pl.multiple_of(first + place, 16), 48), :]
        normed[pl.ds(place, 48), pl.ds(pl.multiple_of(image * KEEP, KEEP), KEEP)] = value.astype(BF)
    out[...] = lax.dot_general(
        slopes[...], normed[...], (((1,), (1,)), ((), ())), preferred_element_type=F32
    )


VMEM = pl.BlockSpec(memory_space=pltpu.VMEM)
SMEM = pl.BlockSpec(memory_space=pltpu.SMEM)


def shards(patches, keep_list, norm_gain, up_weight, hidden_grad):
    dp, mp = lax.axis_index("dp"), lax.axis_index("mp")
    core = dp % 2
    where = jnp.stack([core, jnp.where(core == 0, mp // 16, (mp // 2) % 8), dp]).astype(jnp.int32)

    picked = (lax.broadcasted_iota(jnp.int32, (192, KEEP), 0) == keep_list).astype(BF)
    own = jnp.dot(patches[0].T, picked, preferred_element_type=F32).astype(BF)
    other = lax.ppermute(own, AXES, swap_pairs())
    both = jnp.broadcast_to(jnp.stack([own, other])[None], (16, 2, 48, KEEP))
    both = lax.all_to_all(both, AXES, 0, 0, axis_index_groups=first_groups())
    move = lambda piece, step: lax.ppermute(piece, AXES, ring_pairs(step))
    f2, b1 = move(both, 2), move(both, -1)
    f1, b2 = move(both, 1), move(b1, -1)
    gain_all = pl.pallas_call(
        spread_kernel,
        out_shape=jax.ShapeDtypeStruct((D, KEEP), F32),
        in_specs=[pl.BlockSpec(memory_space=pl.ANY), VMEM],
        out_specs=VMEM,
        compiler_params=pltpu.CompilerParams(vmem_limit_bytes=24 * 2**20),
        cost_estimate=pl.CostEstimate(flops=2 * 2**30, bytes_accessed=8 * 2**20, transcendentals=0),
        name="spread",
    )(b2, norm_gain.reshape(D // 128, 128))
    f3, b3 = move(f2, 1), move(b2, -1)
    f4 = move(f3, 1)
    pieces = (both, f1, f2, f3, f4, b1, b2, b3)

    hidden, payload = pl.pallas_call(
        forward_kernel,
        out_shape=(jax.ShapeDtypeStruct((192, KEEP), BF), jax.ShapeDtypeStruct((4, 208, KEEP), BF)),
        in_specs=[SMEM] + [VMEM] * 11,
        out_specs=(VMEM, VMEM),
        scratch_shapes=[pltpu.VMEM((D, KEEP), BF)],
        compiler_params=pltpu.CompilerParams(vmem_limit_bytes=24 * 2**20),
        name="forward",
    )(where, *pieces, up_weight.T, gain_all, hidden_grad[0].T)

    payload = lax.all_to_all(payload, "dp", 0, 0, axis_index_groups=[[0, 2, 4, 6], [1, 3, 5, 7]])
    payload = lax.all_gather(payload, "dp", axis_index_groups=[[0, 1], [2, 3], [4, 5], [6, 7]])

    grad = pl.pallas_call(
        grad_kernel,
        out_shape=jax.ShapeDtypeStruct((192, 768), F32),
        in_specs=[SMEM] + [VMEM] * 10,
        out_specs=VMEM,
        scratch_shapes=[
            pltpu.VMEM((768, 1024), BF),
            pltpu.VMEM((192, 1024), BF),
            pltpu.VMEM((8, KEEP), F32),
            pltpu.VMEM((8, KEEP), F32),
        ],
        compiler_params=pltpu.CompilerParams(vmem_limit_bytes=24 * 2**20),
        name="weight_grad",
    )(where, *pieces, payload, gain_all)
    return (hidden.T[None], grad.T)


def solution(mesh):
    placed = (P("dp", None, "mp"), P("dp", None), P(), P(None, "mp"), P("dp", None, "mp"))
    return jax.shard_map(
        shards,
        mesh=mesh,
        in_specs=placed,
        out_specs=(P("dp", None, "mp"), P("dp", "mp")),
        check_vma=False,
    )
```

```python
import jax
import jax.numpy as jnp
from jax import lax
from jax.experimental import pallas as pl
from jax.experimental.pallas import tpu as pltpu
from jax.sharding import PartitionSpec as P


epsilon = 1e-06
D = 6144
KEEP = 128
BF = jnp.bfloat16
F32 = jnp.float32
AXES = ("dp", "mp")


def flat(x_hi, core, y, z, x_lo):
    return (x_hi * 2 + core) * 128 + (y % 8) * 16 + (z % 8) * 2 + x_lo


def everyone():
    for x_hi in range(4):
        for core in range(2):
            for y in range(8):
                for z in range(8):
                    for x_lo in range(2):
                        yield x_hi, core, y, z, x_lo


def ring_pairs(step):
    pairs = []
    for x_hi, core, y, z, x_lo in everyone():
        to = (y + step, z) if core == 0 else (y, z + step)
        pairs.append((flat(x_hi, core, y, z, x_lo), flat(x_hi, core, to[0], to[1], x_lo)))
    return pairs


def swap_pairs():
    return [
        (flat(x_hi, core, y, z, x_lo), flat(y // 2, y % 2, x_hi * 2 + core, z, x_lo))
        for x_hi, core, y, z, x_lo in everyone()
    ]


def first_groups():
    groups = []
    for x_hi in range(4):
        for core in range(2):
            for fixed in range(8):
                groups.append(
                    [
                        flat(x_hi, core, *((fixed, run) if core == 0 else (run, fixed)), x_lo)
                        for run in range(8)
                        for x_lo in range(2)
                    ]
                )
    return groups


def gelu_pair(preact):
    normal_cdf = 0.5 * (1.0 + lax.erf(preact * 0.7071067811865476))
    density = jnp.exp(-0.5 * preact * preact) * 0.3989422804014327
    return (preact * normal_cdf, normal_cdf + preact * density)


def tiles(me, pieces, part):
    for shift, ref, places in zip((0, -1, -2, -3, 1, 2, 3, 4, 4), pieces, [range(8)] * 7 + [range(4), range(4, 8)]):
        ring = lax.rem(me + (shift + 8), 8)
        for j in places:
            for half in range(2):
                yield ref.at[2 * (j - places[0]) + half, part], ring, j, half


def spread_kernel(piece, gain, spread):
    for row in range(D // 128):
        spread[row * 128 : (row + 1) * 128, :] = jnp.broadcast_to(gain[row : row + 1, :], (128, KEEP)).T


def forward_kernel(where, *refs):
    pieces = refs[:9]
    weight, gain, hidden_grad, hidden, payload, rows = refs[9:]
    on_y = where[0] == 0
    total = jnp.zeros((8, KEEP), F32)
    for tile, ring, j, half in tiles(where[1], pieces, 0):
        value = tile[...]
        place = jnp.where(on_y, ring * 768 + j * 96, j * 768 + ring * 96) + half * 48
        rows[pl.ds(pl.multiple_of(place, 16), 48), :] = value
        total += jnp.sum(value.astype(F32).reshape(6, 8, KEEP), axis=0)
    average = jnp.sum(total, axis=0, keepdims=True) * (1.0 / D)
    total = jnp.zeros((8, KEEP), F32)
    for start in range(0, D, 256):
        centered = rows[start : start + 256, :].astype(F32) - average
        total += jnp.sum((centered * centered).reshape(32, 8, KEEP), axis=0)
    variance = jnp.sum(total, axis=0, keepdims=True) * (1.0 / D)
    scale = lax.rsqrt(variance + epsilon)
    preact = jnp.zeros((192, KEEP), F32)
    for start in range(0, D, 256):
        centered = rows[start : start + 256, :].astype(F32) - average
        normed = (centered * scale * gain[start : start + 256, :]).astype(BF)
        preact += jnp.dot(weight[:, start : start + 256], normed, preferred_element_type=F32)
    activated, slope_full = gelu_pair(preact)
    hidden[...] = activated.astype(BF)
    slope = (hidden_grad[...].astype(F32) * slope_full).astype(BF)
    lines = []
    for value in (average, scale):
        for _ in range(3):
            top = value.astype(BF).astype(F32)
            lines.append(top)
            value = value - top
    lines.append(jnp.zeros((10, KEEP), F32))
    lines = jnp.concatenate(lines, axis=0).astype(BF)
    for copy in range(4):
        payload[copy, 0:192, :] = slope
        payload[copy, 192:208, :] = lines


def grad_kernel(where, *refs):
    pieces = refs[:9]
    payload, gain, out, normed, slopes, averages, scales = refs[9:]
    first = where[2] * 768
    on_y = where[0] == 0
    for image in range(8):
        ref = payload.at[image % 2, image // 2]
        slopes[:, image * KEEP : (image + 1) * KEEP] = ref[0:192, :]
        lines = ref[192:208, :].astype(F32)
        averages[image : image + 1, :] = lines[0:1] + lines[1:2] + lines[2:3]
        scales[image : image + 1, :] = lines[3:4] + lines[4:5] + lines[5:6]
    for tile, ring, j, half in tiles(where[1], pieces, 1):
        image = jnp.where(on_y, ring, j)
        place = pl.multiple_of(jnp.where(on_y, j * 96, ring * 96) + half * 48, 16)
        centered = tile[...].astype(F32) - averages[pl.ds(image, 1), :]
        value = centered * scales[pl.ds(image, 1), :] * gain[pl.ds(pl.multiple_of(first + place, 16), 48), :]
        normed[pl.ds(place, 48), pl.ds(pl.multiple_of(image * KEEP, KEEP), KEEP)] = value.astype(BF)
    out[...] = lax.dot_general(
        slopes[...], normed[...], (((1,), (1,)), ((), ())), preferred_element_type=F32
    )


VMEM = pl.BlockSpec(memory_space=pltpu.VMEM)
SMEM = pl.BlockSpec(memory_space=pltpu.SMEM)


def shards(patches, keep_list, norm_gain, up_weight, hidden_grad):
    dp, mp = lax.axis_index("dp"), lax.axis_index("mp")
    core = dp % 2
    where = jnp.stack([core, jnp.where(core == 0, mp // 16, (mp // 2) % 8), dp]).astype(jnp.int32)

    picked = (lax.broadcasted_iota(jnp.int32, (192, KEEP), 0) == keep_list).astype(BF)
    own = jnp.dot(patches[0].T, picked, preferred_element_type=F32).astype(BF)
    other = lax.ppermute(own, AXES, swap_pairs())
    both = jnp.broadcast_to(jnp.stack([own, other])[None], (16, 2, 48, KEEP))
    both = lax.all_to_all(both, AXES, 0, 0, axis_index_groups=first_groups())
    move = lambda piece, step: lax.ppermute(piece, AXES, ring_pairs(step))
    f2, b2 = move(both, 2), move(both, -2)
    f1, b1 = move(both, 1), move(both, -1)
    gain_all = pl.pallas_call(
        spread_kernel,
        out_shape=jax.ShapeDtypeStruct((D, KEEP), F32),
        in_specs=[pl.BlockSpec(memory_space=pl.ANY), VMEM],
        out_specs=VMEM,
        compiler_params=pltpu.CompilerParams(vmem_limit_bytes=24 * 2**20),
        cost_estimate=pl.CostEstimate(flops=2 * 2**30, bytes_accessed=8 * 2**20, transcendentals=0),
        name="spread",
    )(b2, norm_gain.reshape(D // 128, 128))
    f3, b3 = move(f2, 1), move(b2, -1)
    f4, b4 = move(f2[:8], 2), move(b2[8:], -2)
    pieces = (both, f1, f2, f3, b1, b2, b3, f4, b4)

    hidden, payload = pl.pallas_call(
        forward_kernel,
        out_shape=(jax.ShapeDtypeStruct((192, KEEP), BF), jax.ShapeDtypeStruct((4, 208, KEEP), BF)),
        in_specs=[SMEM] + [VMEM] * 12,
        out_specs=(VMEM, VMEM),
        scratch_shapes=[pltpu.VMEM((D, KEEP), BF)],
        compiler_params=pltpu.CompilerParams(vmem_limit_bytes=24 * 2**20),
        name="forward",
    )(where, *pieces, up_weight.T, gain_all, hidden_grad[0].T)

    payload = lax.all_to_all(payload, "dp", 0, 0, axis_index_groups=[[0, 2, 4, 6], [1, 3, 5, 7]])
    payload = lax.all_gather(payload, "dp", axis_index_groups=[[0, 1], [2, 3], [4, 5], [6, 7]])

    grad = pl.pallas_call(
        grad_kernel,
        out_shape=jax.ShapeDtypeStruct((192, 768), F32),
        in_specs=[SMEM] + [VMEM] * 11,
        out_specs=VMEM,
        scratch_shapes=[
            pltpu.VMEM((768, 1024), BF),
            pltpu.VMEM((192, 1024), BF),
            pltpu.VMEM((8, KEEP), F32),
            pltpu.VMEM((8, KEEP), F32),
        ],
        compiler_params=pltpu.CompilerParams(vmem_limit_bytes=24 * 2**20),
        name="weight_grad",
    )(where, *pieces, payload, gain_all)
    return (hidden.T[None], grad.T)


def solution(mesh):
    placed = (P("dp", None, "mp"), P("dp", None), P(), P(None, "mp"), P("dp", None, "mp"))
    return jax.shard_map(
        shards,
        mesh=mesh,
        in_specs=placed,
        out_specs=(P("dp", None, "mp"), P("dp", "mp")),
        check_vma=False,
    )
```

```python
import jax
import jax.numpy as jnp
from jax import lax
from jax.experimental import pallas as pl
from jax.experimental.pallas import tpu as pltpu
from jax.sharding import PartitionSpec as P


epsilon = 1e-06
D = 6144
KEEP = 128
BF = jnp.bfloat16
F32 = jnp.float32
AXES = ("dp", "mp")


def flat(x_hi, core, y, z, x_lo):
    return (x_hi * 2 + core) * 128 + (y % 8) * 16 + (z % 8) * 2 + x_lo


def everyone():
    for x_hi in range(4):
        for core in range(2):
            for y in range(8):
                for z in range(8):
                    for x_lo in range(2):
                        yield x_hi, core, y, z, x_lo


def ring_pairs(step):
    pairs = []
    for x_hi, core, y, z, x_lo in everyone():
        to = (y + step, z) if core == 0 else (y, z + step)
        pairs.append((flat(x_hi, core, y, z, x_lo), flat(x_hi, core, to[0], to[1], x_lo)))
    return pairs


def swap_pairs():
    return [
        (flat(x_hi, core, y, z, x_lo), flat(y // 2, y % 2, x_hi * 2 + core, z, x_lo))
        for x_hi, core, y, z, x_lo in everyone()
    ]


def first_groups():
    groups = []
    for x_hi in range(4):
        for core in range(2):
            for fixed in range(8):
                groups.append(
                    [
                        flat(x_hi, core, *((fixed, run) if core == 0 else (run, fixed)), x_lo)
                        for run in range(8)
                        for x_lo in range(2)
                    ]
                )
    return groups


def gelu_pair(preact):
    normal_cdf = 0.5 * (1.0 + lax.erf(preact * 0.7071067811865476))
    density = jnp.exp(-0.5 * preact * preact) * 0.3989422804014327
    return (preact * normal_cdf, normal_cdf + preact * density)


def tiles(me, pieces, part):
    for shift, ref in zip((0, -1, -2, -3, 1, 2, 3, 4), pieces):
        ring = lax.rem(me + (shift + 8), 8)
        for j in range(8):
            for half in range(2):
                yield ref.at[2 * j + half] if shift == 4 or part == 1 else ref.at[2 * j + half, 0], ring, j, half


def part_kernel(part, bundle, out):
    out[...] = bundle[:, part]


def spread_kernel(piece, gain, spread):
    for row in range(D // 128):
        spread[row * 128 : (row + 1) * 128, :] = jnp.broadcast_to(gain[row : row + 1, :], (128, KEEP)).T


def forward_kernel(where, *refs):
    pieces = refs[:8]
    weight, gain, hidden_grad, hidden, payload, rows = refs[8:]
    on_y = where[0] == 0
    total = jnp.zeros((8, KEEP), F32)
    for tile, ring, j, half in tiles(where[1], pieces, 0):
        value = tile[...]
        place = jnp.where(on_y, ring * 768 + j * 96, j * 768 + ring * 96) + half * 48
        rows[pl.ds(pl.multiple_of(place, 16), 48), :] = value
        total += jnp.sum(value.astype(F32).reshape(6, 8, KEEP), axis=0)
    average = jnp.sum(total, axis=0, keepdims=True) * (1.0 / D)
    total = jnp.zeros((8, KEEP), F32)
    for start in range(0, D, 256):
        centered = rows[start : start + 256, :].astype(F32) - average
        total += jnp.sum((centered * centered).reshape(32, 8, KEEP), axis=0)
    variance = jnp.sum(total, axis=0, keepdims=True) * (1.0 / D)
    scale = lax.rsqrt(variance + epsilon)
    preact = jnp.zeros((192, KEEP), F32)
    for start in range(0, D, 256):
        centered = rows[start : start + 256, :].astype(F32) - average
        normed = (centered * scale * gain[start : start + 256, :]).astype(BF)
        preact += jnp.dot(weight[:, start : start + 256], normed, preferred_element_type=F32)
    activated, slope_full = gelu_pair(preact)
    hidden[...] = activated.astype(BF)
    slope = (hidden_grad[...].astype(F32) * slope_full).astype(BF)
    lines = []
    for value in (average, scale):
        for _ in range(3):
            top = value.astype(BF).astype(F32)
            lines.append(top)
            value = value - top
    lines.append(jnp.zeros((10, KEEP), F32))
    lines = jnp.concatenate(lines, axis=0).astype(BF)
    for copy in range(4):
        payload[copy, 0:192, :] = slope
        payload[copy, 192:208, :] = lines


def grad_kernel(where, *refs):
    payload, gain, out, normed, slopes, averages, scales, landed, arrived = refs[8:]
    copies = []
    for k in range(8):
        source = refs[k] if k == 7 else refs[k].at[:, 1]
        copies.append(pltpu.make_async_copy(source, landed.at[k], arrived.at[k]))
        copies[k].start()
    pieces = [landed.at[k] for k in range(8)]
    first = where[2] * 768
    on_y = where[0] == 0
    for image in range(8):
        ref = payload.at[image % 2, image // 2]
        slopes[:, image * KEEP : (image + 1) * KEEP] = ref[0:192, :]
        lines = ref[192:208, :].astype(F32)
        averages[image : image + 1, :] = lines[0:1] + lines[1:2] + lines[2:3]
        scales[image : image + 1, :] = lines[3:4] + lines[4:5] + lines[5:6]
    for copy in copies:
        copy.wait()
    for tile, ring, j, half in tiles(where[1], pieces, 1):
        image = jnp.where(on_y, ring, j)
        place = pl.multiple_of(jnp.where(on_y, j * 96, ring * 96) + half * 48, 16)
        centered = tile[...].astype(F32) - averages[pl.ds(image, 1), :]
        value = centered * scales[pl.ds(image, 1), :] * gain[pl.ds(pl.multiple_of(first + place, 16), 48), :]
        normed[pl.ds(place, 48), pl.ds(pl.multiple_of(image * KEEP, KEEP), KEEP)] = value.astype(BF)
    out[...] = lax.dot_general(
        slopes[...], normed[...], (((1,), (1,)), ((), ())), preferred_element_type=F32
    )


VMEM = pl.BlockSpec(memory_space=pltpu.VMEM)
SMEM = pl.BlockSpec(memory_space=pltpu.SMEM)
ANY = pl.BlockSpec(memory_space=pltpu.HBM)


def part_of(part, bundle):
    return pl.pallas_call(
        lambda *refs: part_kernel(part, *refs),
        out_shape=jax.ShapeDtypeStruct((16, 48, KEEP), BF),
        in_specs=[VMEM],
        out_specs=VMEM,
        compiler_params=pltpu.CompilerParams(vmem_limit_bytes=24 * 2**20),
        name="own_part" if part == 0 else "other_part",
    )(bundle)


def shards(patches, keep_list, norm_gain, up_weight, hidden_grad):
    dp, mp = lax.axis_index("dp"), lax.axis_index("mp")
    core = dp % 2
    where = jnp.stack([core, jnp.where(core == 0, mp // 16, (mp // 2) % 8), dp]).astype(jnp.int32)

    picked = (lax.broadcasted_iota(jnp.int32, (192, KEEP), 0) == keep_list).astype(BF)
    own = jnp.dot(patches[0].T, picked, preferred_element_type=F32).astype(BF)
    other = lax.ppermute(own, AXES, swap_pairs())
    both = jnp.broadcast_to(jnp.stack([own, other])[None], (16, 2, 48, KEEP))
    both = lax.all_to_all(both, AXES, 0, 0, axis_index_groups=first_groups())
    move = lambda piece, step: lax.ppermute(piece, AXES, ring_pairs(step))
    f2, b2 = move(both, 2), move(both, -2)
    f1, b1 = move(both, 1), move(both, -1)
    gain_all = pl.pallas_call(
        spread_kernel,
        out_shape=jax.ShapeDtypeStruct((D, KEEP), F32),
        in_specs=[pl.BlockSpec(memory_space=pl.ANY), VMEM],
        out_specs=VMEM,
        compiler_params=pltpu.CompilerParams(vmem_limit_bytes=24 * 2**20),
        cost_estimate=pl.CostEstimate(flops=2 * 2**30, bytes_accessed=8 * 2**20, transcendentals=0),
        name="spread",
    )(b2, norm_gain.reshape(D // 128, 128))
    f3, b3 = move(f2, 1), move(b2, -1)
    f4, b4 = move(part_of(0, f2), 2), move(part_of(1, b2), -2)
    pieces = (both, f1, f2, f3, b1, b2, b3)

    hidden, payload = pl.pallas_call(
        forward_kernel,
        out_shape=(jax.ShapeDtypeStruct((192, KEEP), BF), jax.ShapeDtypeStruct((4, 208, KEEP), BF)),
        in_specs=[SMEM] + [VMEM] * 11,
        out_specs=(VMEM, VMEM),
        scratch_shapes=[pltpu.VMEM((D, KEEP), BF)],
        compiler_params=pltpu.CompilerParams(vmem_limit_bytes=24 * 2**20),
        name="forward",
    )(where, *pieces, f4, up_weight.T, gain_all, hidden_grad[0].T)

    payload = lax.all_to_all(payload, "dp", 0, 0, axis_index_groups=[[0, 2, 4, 6], [1, 3, 5, 7]])
    payload = lax.all_gather(payload, "dp", axis_index_groups=[[0, 1], [2, 3], [4, 5], [6, 7]])

    grad = pl.pallas_call(
        grad_kernel,
        out_shape=jax.ShapeDtypeStruct((192, 768), F32),
        in_specs=[SMEM] + [ANY] * 8 + [VMEM] * 2,
        out_specs=VMEM,
        scratch_shapes=[
            pltpu.VMEM((768, 1024), BF),
            pltpu.VMEM((192, 1024), BF),
            pltpu.VMEM((8, KEEP), F32),
            pltpu.VMEM((8, KEEP), F32),
            pltpu.VMEM((8, 16, 48, KEEP), BF),
            pltpu.SemaphoreType.DMA((8,)),
        ],
        compiler_params=pltpu.CompilerParams(vmem_limit_bytes=24 * 2**20),
        name="weight_grad",
    )(where, *pieces, b4, payload, gain_all)
    return (hidden.T[None], grad.T)


def solution(mesh):
    placed = (P("dp", None, "mp"), P("dp", None), P(), P(None, "mp"), P("dp", None, "mp"))
    return jax.shard_map(
        shards,
        mesh=mesh,
        in_specs=placed,
        out_specs=(P("dp", None, "mp"), P("dp", "mp")),
        check_vma=False,
    )
```

```python
import jax
import jax.numpy as jnp
from jax import lax
from jax.experimental import pallas as pl
from jax.experimental.pallas import tpu as pltpu
from jax.sharding import PartitionSpec as P


epsilon = 1e-06
D = 6144
KEEP = 128
BF = jnp.bfloat16
F32 = jnp.float32
AXES = ("dp", "mp")


def flat(x_hi, core, y, z, x_lo):
    return (x_hi * 2 + core) * 128 + (y % 8) * 16 + (z % 8) * 2 + x_lo


def everyone():
    for x_hi in range(4):
        for core in range(2):
            for y in range(8):
                for z in range(8):
                    for x_lo in range(2):
                        yield x_hi, core, y, z, x_lo


def ring_pairs(step):
    pairs = []
    for x_hi, core, y, z, x_lo in everyone():
        to = (y + step, z) if core == 0 else (y, z + step)
        pairs.append((flat(x_hi, core, y, z, x_lo), flat(x_hi, core, to[0], to[1], x_lo)))
    return pairs


def swap_pairs():
    return [
        (flat(x_hi, core, y, z, x_lo), flat(y // 2, y % 2, x_hi * 2 + core, z, x_lo))
        for x_hi, core, y, z, x_lo in everyone()
    ]


def first_groups():
    groups = []
    for x_hi in range(4):
        for core in range(2):
            for fixed in range(8):
                groups.append(
                    [
                        flat(x_hi, core, *((fixed, run) if core == 0 else (run, fixed)), x_lo)
                        for run in range(8)
                        for x_lo in range(2)
                    ]
                )
    return groups


def gelu_pair(preact):
    normal_cdf = 0.5 * (1.0 + lax.erf(preact * 0.7071067811865476))
    density = jnp.exp(-0.5 * preact * preact) * 0.3989422804014327
    return (preact * normal_cdf, normal_cdf + preact * density)


def tiles(me, pieces, part):
    for shift, ref, places in zip((0, -1, -2, -3, 1, 2, 3, 4, 4), pieces, [range(8)] * 7 + [range(4), range(4, 8)]):
        ring = lax.rem(me + (shift + 8), 8)
        for j in places:
            for half in range(2):
                yield ref.at[2 * (j - places[0]) + half, part], ring, j, half


def spread_kernel(piece, gain, spread):
    for row in range(D // 128):
        spread[row * 128 : (row + 1) * 128, :] = jnp.broadcast_to(gain[row : row + 1, :], (128, KEEP)).T


def forward_kernel(where, *refs):
    pieces = refs[:9]
    weight, gain, hidden_grad, hidden, payload, rows = refs[9:]
    on_y = where[0] == 0
    total = jnp.zeros((8, KEEP), F32)
    for tile, ring, j, half in tiles(where[1], pieces, 0):
        value = tile[...]
        place = jnp.where(on_y, ring * 768 + j * 96, j * 768 + ring * 96) + half * 48
        rows[pl.ds(pl.multiple_of(place, 16), 48), :] = value
        total += jnp.sum(value.astype(F32).reshape(6, 8, KEEP), axis=0)
    average = jnp.sum(total, axis=0, keepdims=True) * (1.0 / D)
    total = jnp.zeros((8, KEEP), F32)
    for start in range(0, D, 256):
        centered = rows[start : start + 256, :].astype(F32) - average
        total += jnp.sum((centered * centered).reshape(32, 8, KEEP), axis=0)
    variance = jnp.sum(total, axis=0, keepdims=True) * (1.0 / D)
    scale = lax.rsqrt(variance + epsilon)
    preact = jnp.zeros((192, KEEP), F32)
    for start in range(0, D, 256):
        centered = rows[start : start + 256, :].astype(F32) - average
        normed = (centered * scale * gain[start : start + 256, :]).astype(BF)
        preact += jnp.dot(weight[:, start : start + 256], normed, preferred_element_type=F32)
    activated, slope_full = gelu_pair(preact)
    hidden[...] = activated.astype(BF)
    slope = (hidden_grad[...].astype(F32) * slope_full).astype(BF)
    lines = []
    for value in (average, scale):
        for _ in range(3):
            top = value.astype(BF).astype(F32)
            lines.append(top)
            value = value - top
    lines.append(jnp.zeros((10, KEEP), F32))
    lines = jnp.concatenate(lines, axis=0).astype(BF)
    payload[0:192, :] = slope
    payload[192:208, :] = lines


def grad_kernel(where, *refs):
    pieces = refs[:9]
    payload, gain, out, normed, slopes, averages, scales = refs[9:]
    first = where[2] * 768
    on_y = where[0] == 0
    for image in range(8):
        ref = payload.at[image]
        slopes[:, image * KEEP : (image + 1) * KEEP] = ref[0:192, :]
        lines = ref[192:208, :].astype(F32)
        averages[image : image + 1, :] = lines[0:1] + lines[1:2] + lines[2:3]
        scales[image : image + 1, :] = lines[3:4] + lines[4:5] + lines[5:6]
    for tile, ring, j, half in tiles(where[1], pieces, 1):
        image = jnp.where(on_y, ring, j)
        place = pl.multiple_of(jnp.where(on_y, j * 96, ring * 96) + half * 48, 16)
        centered = tile[...].astype(F32) - averages[pl.ds(image, 1), :]
        value = centered * scales[pl.ds(image, 1), :] * gain[pl.ds(pl.multiple_of(first + place, 16), 48), :]
        normed[pl.ds(place, 48), pl.ds(pl.multiple_of(image * KEEP, KEEP), KEEP)] = value.astype(BF)
    out[...] = lax.dot_general(
        slopes[...], normed[...], (((1,), (1,)), ((), ())), preferred_element_type=F32
    )


VMEM = pl.BlockSpec(memory_space=pltpu.VMEM)
SMEM = pl.BlockSpec(memory_space=pltpu.SMEM)


def shards(patches, keep_list, norm_gain, up_weight, hidden_grad):
    dp, mp = lax.axis_index("dp"), lax.axis_index("mp")
    core = dp % 2
    where = jnp.stack([core, jnp.where(core == 0, mp // 16, (mp // 2) % 8), dp]).astype(jnp.int32)

    picked = (lax.broadcasted_iota(jnp.int32, (192, KEEP), 0) == keep_list).astype(BF)
    own = jnp.dot(patches[0].T, picked, preferred_element_type=F32).astype(BF)
    other = lax.ppermute(own, AXES, swap_pairs())
    both = jnp.broadcast_to(jnp.stack([own, other])[None], (16, 2, 48, KEEP))
    both = lax.all_to_all(both, AXES, 0, 0, axis_index_groups=first_groups())
    move = lambda piece, step: lax.ppermute(piece, AXES, ring_pairs(step))
    f2, b2 = move(both, 2), move(both, -2)
    f1, b1 = move(both, 1), move(both, -1)
    gain_all = pl.pallas_call(
        spread_kernel,
        out_shape=jax.ShapeDtypeStruct((D, KEEP), F32),
        in_specs=[pl.BlockSpec(memory_space=pl.ANY), VMEM],
        out_specs=VMEM,
        compiler_params=pltpu.CompilerParams(vmem_limit_bytes=24 * 2**20),
        cost_estimate=pl.CostEstimate(flops=2 * 2**30, bytes_accessed=8 * 2**20, transcendentals=0),
        name="spread",
    )(b2, norm_gain.reshape(D // 128, 128))
    f3, b3 = move(f2, 1), move(b2, -1)
    f4, b4 = move(f2[:8], 2), move(b2[8:], -2)
    pieces = (both, f1, f2, f3, b1, b2, b3, f4, b4)

    hidden, payload = pl.pallas_call(
        forward_kernel,
        out_shape=(jax.ShapeDtypeStruct((192, KEEP), BF), jax.ShapeDtypeStruct((208, KEEP), BF)),
        in_specs=[SMEM] + [VMEM] * 12,
        out_specs=(VMEM, VMEM),
        scratch_shapes=[pltpu.VMEM((D, KEEP), BF)],
        compiler_params=pltpu.CompilerParams(vmem_limit_bytes=24 * 2**20),
        name="forward",
    )(where, *pieces, up_weight.T, gain_all, hidden_grad[0].T)

    payload = lax.all_gather(payload, "dp")

    grad = pl.pallas_call(
        grad_kernel,
        out_shape=jax.ShapeDtypeStruct((192, 768), F32),
        in_specs=[SMEM] + [VMEM] * 11,
        out_specs=VMEM,
        scratch_shapes=[
            pltpu.VMEM((768, 1024), BF),
            pltpu.VMEM((192, 1024), BF),
            pltpu.VMEM((8, KEEP), F32),
            pltpu.VMEM((8, KEEP), F32),
        ],
        compiler_params=pltpu.CompilerParams(vmem_limit_bytes=24 * 2**20),
        name="weight_grad",
    )(where, *pieces, payload, gain_all)
    return (hidden.T[None], grad.T)


def solution(mesh):
    placed = (P("dp", None, "mp"), P("dp", None), P(), P(None, "mp"), P("dp", None, "mp"))
    return jax.shard_map(
        shards,
        mesh=mesh,
        in_specs=placed,
        out_specs=(P("dp", None, "mp"), P("dp", "mp")),
        check_vma=False,
    )
```
